512 devices in a mesh: sweep: 16 (over z_lo, core), dof: 32 (over y, x, z_hi).
Axes of the slice: x: 4, y: 4, z: 16 (z_hi: 2, z_lo: 8; z = z_hi * 8 + z_lo), core: 2. Of those that a mesh axis runs over, the one named last changes fastest.
Arguments:
- mode_shapes: bfloat16 [32, 3, 10240, 256], P('sweep', None, 'dof'), may hold values from -6 to 6
- mass_blocks: float32 [3, 3, 8, 10240], P(None, None, None, 'dof'), may hold values from -0.01171875 to 0.01171875
- block_cols: int32 [8, 10240], P(None, 'dof'), may hold values from 0 to 575, as said below
- send_lists: int32 [32, 2, 128], P('dof'), may hold values from 0 to 319, as said below
Outputs:
- margins: float32 [256, 32, 256], P('dof', 'sweep')
The draws below stay inside these ranges and needn't reach their ends.
Inputs may be any that keep to these rules, and one draw needn't show every extreme that they name: `block_cols`: slot 0 of node n's block row is the node itself (n modulo 320); other slots point anywhere in the extended list of 576 nodes. `send_lists`: local node indices of the sending partition.
All inputs are finite; a program needn't handle non-finite values.
Results may differ from the reference program's by a relative error of at most 0.0029.
Values may be sent and summed in bfloat16 or wider, within the bound.
A program may use at most 64 MiB of HBM per device.

```python
import jax
import jax.numpy as jnp
from jax import lax

K = 256
NODE_DEV = 320
HALO = 128
BLOCKS = 8
STEPS = 32
NODES = 10240
NPART = 32


def draw_block_cols(key, part):
    key = jax.random.fold_in(key, 11)
    own_nodes = (jnp.arange(NODES, dtype=jnp.int32) % NODE_DEV)[None]
    others = jax.random.randint(key, (BLOCKS - 1, NODES), 0, NODE_DEV + 2 * HALO, dtype=jnp.int32)
    others = others.at[BLOCKS - 2, NODES - 1].set(NODE_DEV + 2 * HALO - 1)
    return jnp.concatenate([own_nodes, others], axis=0)


def draw_send_lists(key, part):
    key = jax.random.fold_in(key, 23)
    keys_all = jax.random.split(key, NPART * 2)
    chosen = jax.vmap(lambda subkey: jax.random.permutation(subkey, NODE_DEV)[:HALO])(keys_all)
    chosen = chosen.reshape(NPART, 2, HALO).astype(jnp.int32)
    chosen = chosen.at[0, 0, 0].set(NODE_DEV - 1).at[0, 1, 0].set(0)
    return chosen


def steps_of(rng, shape, shards, least, top_value):
    def one(dim, parts):
        heights = jax.random.uniform(jax.random.fold_in(jax.random.fold_in(rng, 6), dim), (parts,), jnp.float32, least / len(shards), top_value / len(shards))
        return jnp.repeat(jnp.exp(heights), shape[dim] // parts).reshape((-1,) + (1,) * (len(shape) - dim - 1))

    factor_of = one(*shards[0])
    for cut in shards[1:]:
        factor_of = factor_of * one(*cut)
    return factor_of


def gaussian(rng, shape, width, most, cuts=(), held_as=jnp.bfloat16):
    entries = jax.random.normal(rng, shape, jnp.float32) * width
    if len(cuts) > 0:
        entries = steps_of(rng, shape, cuts, -0.22, 0.18) * entries
    return jnp.clip(entries, min=-most, max=most).astype(held_as)


def setup_inputs(seed: int = 0) -> dict:
    keys = jax.random.split(jax.random.key(seed), 5)
    return {
        "mode_shapes": gaussian(keys[0], (STEPS, 3, NODES, K), 1.0, 6.0, ((0, 16), (2, 32))),
        "mass_blocks": gaussian(keys[1], (3, 3, BLOCKS, NODES), (3 * BLOCKS * NODES) ** -0.5, 0.01171875, ((3, 32),), jnp.float32),
        "block_cols": draw_block_cols(jax.random.fold_in(keys[4], 71), 0),
        "send_lists": draw_send_lists(jax.random.fold_in(keys[4], 71), 0),
    }


def apply_mass(field, send_lists, block_cols, mass_blocks):
    partitions = send_lists.shape[0]
    modes_count = field.shape[2]
    node_width = field.shape[1] // partitions
    shaped = field.reshape(3, partitions, node_width, modes_count)
    part_index = jnp.arange(partitions, dtype=jnp.int32)[:, None]
    to_right = shaped[:, part_index, send_lists[:, 0, :]]
    to_left = shaped[:, part_index, send_lists[:, 1, :]]
    extended = jnp.concatenate([shaped, jnp.roll(to_right, 1, axis=1), jnp.roll(to_left, -1, axis=1)], axis=2)
    columns_all = block_cols.reshape(block_cols.shape[0], partitions, node_width)
    masses = mass_blocks.reshape(3, 3, block_cols.shape[0], partitions, node_width)
    running = jnp.zeros(shaped.shape, jnp.float32)
    for column in range(columns_all.shape[0]):
        gathered = extended[:, part_index, columns_all[column]].astype(jnp.float32)
        for component in range(3):
            running = running + masses[:, component, column][..., None] * gathered[component][None]
    return running.astype(jnp.bfloat16).reshape(field.shape)


def reference(mode_shapes, mass_blocks, block_cols, send_lists):
    steps_total = mode_shapes.shape[0]
    modes_count = mode_shapes.shape[3]

    def margin_pair(step_index):
        next_step = jnp.minimum(step_index + 1, steps_total - 1)
        earlier = mode_shapes[step_index]
        mass_image = apply_mass(mode_shapes[next_step], send_lists, block_cols, mass_blocks)
        return jnp.dot(earlier.reshape(-1, modes_count).T, mass_image.reshape(-1, modes_count), preferred_element_type=jnp.float32)

    margins = lax.map(margin_pair, jnp.arange(steps_total, dtype=jnp.int32))
    return jnp.transpose(margins, (1, 0, 2))
```

```python
import jax
import jax.numpy as jnp
from jax import lax
from jax.experimental import pallas as pl
from jax.experimental.pallas import tpu as pltpu
from jax.sharding import PartitionSpec as P

MESH = pl.DeviceIdType.MESH
F32, BF16 = jnp.float32, jnp.bfloat16
HALVES = 2


def dot(a, b):
    return jnp.dot(a, b, preferred_element_type=F32)


def dot_t(a, b):
    return lax.dot_general(a, b, (((0,), (0,)), ((), ())), preferred_element_type=F32)


def margins_kernel(n_sweep, n_dof, modes, mass, cols, lists, out, fq, fr, cb, pk_own, pk_q, pk_r, cols3, mt_hi, mt_lo,
                   mq_hi, mq_lo, mr_hi, mr_lo, ya_own, ya_halo, yb, gt_q, gt_r, cs_q, cs_r, part, acc_bt, rsb, tot, last,
                   z_ss, z_rs, x_ss, x_rs, m_ss, m_rs, r_ss, r_rs):
    nodes, halo, width = cols.shape[1], lists.shape[2], modes.shape[2]
    rows = 3 * nodes
    planes = n_dof // 2
    z_lo_n = n_sweep // 2
    half = width // HALVES
    w, p = lax.axis_index("sweep"), lax.axis_index("dof")
    core, z_lo = lax.rem(w, 2), w // 2
    k, z_hi = p // 2, lax.rem(p, 2)
    far = {"dof": 2 * k + (1 - z_hi)}

    def plane(kk):
        return {"dof": 2 * lax.rem(kk + planes, planes) + z_hi}

    def z_step(by):
        moved = z_lo + by
        wrapped = jnp.logical_or(moved < 0, moved >= z_lo_n)
        lo = lax.rem(moved + z_lo_n, z_lo_n)
        hi = jnp.where(wrapped, 1 - z_hi, z_hi)
        return {"sweep": lo * 2 + core, "dof": 2 * k + hi}

    def sweep_step(by):
        return {"sweep": lax.rem(w + by + n_sweep, n_sweep)}

    towards = jnp.where(z_lo < z_lo_n // 2, 1, -1)
    depth = jnp.where(z_lo < z_lo_n // 2, z_lo, z_lo_n - 1 - z_lo)
    is_first, is_last = w == 0, w == n_sweep - 1

    barrier = pltpu.get_barrier_semaphore()
    greeted = [far, sweep_step(1), sweep_step(-1), z_step(1), z_step(-1)]
    greeted += [plane(k + t) for t in range(1, planes)]
    for device in greeted:
        pl.semaphore_signal(barrier, inc=1, device_id=device, device_id_type=MESH)
    pl.semaphore_wait(barrier, len(greeted))

    def remote(src, dst, send, recv, device):
        return pltpu.make_async_remote_copy(src_ref=src, dst_ref=dst, send_sem=send, recv_sem=recv, device_id=device,
                                            device_id_type=MESH)

    chunks = [(c, h) for h in range(HALVES) for c in range(3)]

    def piece(ref, c, h):
        return ref.at[pl.ds(c * nodes, nodes), pl.ds(h * half, half)]

    x_next = plane(k + 1 - 2 * z_hi)
    z_copies = [remote(piece(modes.at[1], c, h), piece(fq, c, h), z_ss.at[i], z_rs.at[i], far) for i, (c, h) in enumerate(chunks)]
    x_copies = [remote(piece(fq, c, h), piece(fr, c, h), x_ss.at[i], x_rs.at[i], x_next) for i, (c, h) in enumerate(chunks)]
    for copy in z_copies:
        copy.start()
    c_copy = remote(modes.at[0], cb, m_ss.at[0], m_rs.at[0], sweep_step(-1))

    @pl.when(w > 0)
    def _():
        c_copy.start()

    for d in range(3):
        pk_own[d] = jnp.concatenate([mass[c, d] for c in range(3)], axis=1)
    pk_own[3, :, 0:nodes] = cols[...].astype(F32)
    pk_own[3, 0:2, 384:384 + halo] = lists[0].astype(F32)

    mine = pl.ds(2 * core, 2)
    own_copy = remote(pk_own.at[mine], pk_q.at[mine], m_ss.at[1], m_rs.at[1], z_step(-towards))
    chain_copy = remote(pk_q.at[mine], pk_q.at[mine], m_ss.at[2], m_rs.at[1], z_step(towards))
    core_copy = remote(pk_q.at[mine], pk_q.at[mine], m_ss.at[3], m_rs.at[2], {"sweep": z_lo * 2 + 1 - core})
    pack_copy = remote(pk_q, pk_r, m_ss.at[4], m_rs.at[3], x_next)

    @pl.when(depth == 0)
    def _():
        own_copy.start()

    def build(pk, offset, count, hi, lo):
        one = pk[3, :, 0:nodes]
        cols3[...] = jnp.concatenate([one, one, one], axis=1)

        def body(g, carry):
            r = pl.multiple_of(g * 16, 16)
            for lane, lanes in ((0, 512), (512, rows - 512)):
                ids = (lax.broadcasted_iota(jnp.int32, (16, lanes), 0) + (r + offset)).astype(F32)
                sums = [jnp.zeros((16, lanes), F32) for _ in range(3)]
                for b in range(8):
                    hit = ids == cols3[b:b + 1, lane:lane + lanes]
                    for d in range(3):
                        sums[d] = sums[d] + jnp.where(hit, pk[d, b:b + 1, lane:lane + lanes], 0.0)
                for d in range(3):
                    top = sums[d].astype(BF16)
                    hi[d, pl.ds(r, 16), lane:lane + lanes] = top
                    lo[d, pl.ds(r, 16), lane:lane + lanes] = (sums[d] - top.astype(F32)).astype(BF16)
            return carry

        lax.fori_loop(0, count // 16, body, 0)

    def one_hot(row):
        ids = lax.broadcasted_iota(jnp.int32, (nodes, halo), 0).astype(F32)
        return jnp.where(ids == row, 1.0, 0.0).astype(BF16)

    build(pk_own, 0, nodes + 2 * halo, mt_hi, mt_lo)

    own_copy.wait_recv()

    @pl.when(depth < z_lo_n // 2 - 1)
    def _():
        chain_copy.start()

    core_copy.start()

    for d in range(3):
        first = dot(mt_hi[d], modes[0]) + dot(mt_lo[d], modes[0])
        ya_own[pl.ds(d * nodes, nodes), :] = first[0:nodes].astype(BF16)
        ya_halo[d] = first[nodes:].astype(BF16)
    part[0] = dot_t(ya_own[...], modes[1])

    core_copy.wait_recv()
    pack_copy.start()

    for d in range(3):
        second = dot(mt_hi[d, 0:nodes], modes[1]) + dot(mt_lo[d, 0:nodes], modes[1])
        yb[pl.ds(d * nodes, nodes), :] = second.astype(BF16)

    @pl.when(jnp.logical_not(is_last))
    def _():
        c_copy.wait_recv()

    @pl.when(is_last)
    def _():
        cb[...] = modes[1]

    acc_bt[...] = dot_t(cb[...], yb[...])

    def side(pk, seg_here, row_there, seg_there, row_here, hi, lo, gt, cs):
        there = one_hot(jnp.where(row_there == 0, pk[3, 0:1, 384:384 + halo], pk[3, 1:2, 384:384 + halo]))
        here = one_hot(jnp.where(row_here == 0, lists[0, 0:1, :], lists[0, 1:2, :]).astype(F32))
        build(pk, nodes + halo * seg_there, halo, hi, lo)
        for d in range(3):
            gt[pl.ds(d * nodes, nodes), :] = dot(there, ya_halo[d, pl.ds(pl.multiple_of(halo * seg_here, halo), halo), :]).astype(BF16)
            cs[pl.ds(d * halo, halo), :] = dot_t(here, cb[pl.ds(d * nodes, nodes), :]).astype(BF16)

    def use(field, hi, lo, gt, cs, h):
        lanes = slice(h * half, (h + 1) * half)
        block = field[:, lanes]
        y = (dot(hi[...].reshape(3 * halo, rows), block) + dot(lo[...].reshape(3 * halo, rows), block)).astype(BF16)
        acc_bt[:, lanes] += dot_t(cs[...], y)
        part[0, :, lanes] += dot_t(gt[...], block)

    side(pk_q, 1 - z_hi, 1 - z_hi, z_hi, z_hi, mq_hi, mq_lo, gt_q, cs_q)
    z_copies[0].wait_recv()
    x_copies[0].start()
    pack_copy.wait_recv()
    side(pk_r, z_hi, z_hi, 1 - z_hi, 1 - z_hi, mr_hi, mr_lo, gt_r, cs_r)

    for h in range(HALVES):
        for i, (c, hh) in enumerate(chunks):
            if hh == h and i > 0:
                z_copies[i].wait_recv()
                x_copies[i].start()
        use(fq, mq_hi, mq_lo, gt_q, cs_q, h)
        for i, (c, hh) in enumerate(chunks):
            if hh == h:
                x_copies[i].wait_recv()
        use(fr, mr_hi, mr_lo, gt_r, cs_r, h)

    part[1] = acc_bt[...].T

    share = width // n_dof
    pair = 2 * share
    sends = []
    for t in range(1, planes):
        there = lax.rem(k + t, planes)
        sends.append(remote(part.at[:, pl.ds(pl.multiple_of(there * pair, pair), pair), :], rsb.at[t - 1], r_ss.at[t - 1],
                            r_rs.at[t - 1], plane(k + t)))
    for copy in sends:
        copy.start()
    total = part[:, pl.ds(pl.multiple_of(k * pair, pair), pair), :]
    for t, copy in enumerate(sends):
        copy.wait_recv()
        total = total + rsb[t]
    tot[:, 0] = total[:, 0:share]
    tot[:, 1] = total[:, share:]
    last_copy = remote(tot.at[:, 1 - z_hi], last, m_ss.at[5], m_rs.at[4], far)
    last_copy.start()

    for copy in z_copies + x_copies + sends:
        copy.wait_send()

    @pl.when(w > 0)
    def _():
        c_copy.wait_send()

    @pl.when(depth == 0)
    def _():
        own_copy.wait_send()

    @pl.when(depth < z_lo_n // 2 - 1)
    def _():
        chain_copy.wait_send()

    core_copy.wait_send()
    pack_copy.wait_send()
    last_copy.wait()
    for s in range(2):
        out[:, s, :] = tot[s, pl.ds(z_hi, 1)][0] + last[s]


def solution(mesh):
    n_sweep, n_dof = mesh.shape["sweep"], mesh.shape["dof"]

    def local(mode_shapes, mass_blocks, block_cols, send_lists):
        _, _, nodes, width = mode_shapes.shape
        halo = send_lists.shape[2]
        rows, planes, share = 3 * nodes, n_dof // 2, width // n_dof
        ext = nodes + 2 * halo
        vmem = pltpu.VMEM
        dma = pltpu.SemaphoreType.DMA
        return pl.pallas_call(
            lambda *refs: margins_kernel(n_sweep, n_dof, *refs),
            out_shape=jax.ShapeDtypeStruct((share, 2, width), F32),
            in_specs=[pl.BlockSpec(memory_space=pltpu.VMEM)] * 4,
            out_specs=pl.BlockSpec(memory_space=pltpu.VMEM),
            scratch_shapes=[
                vmem((rows, width), BF16), vmem((rows, width), BF16), vmem((rows, width), BF16),
                vmem((4, 8, rows), F32), vmem((4, 8, rows), F32), vmem((4, 8, rows), F32), vmem((8, rows), F32),
                vmem((3, ext, rows), BF16), vmem((3, ext, rows), BF16),
                vmem((3, halo, rows), BF16), vmem((3, halo, rows), BF16),
                vmem((3, halo, rows), BF16), vmem((3, halo, rows), BF16),
                vmem((rows, width), BF16), vmem((3, 2 * halo, width), BF16), vmem((rows, width), BF16),
                vmem((rows, width), BF16), vmem((rows, width), BF16),
                vmem((3 * halo, width), BF16), vmem((3 * halo, width), BF16),
                vmem((2, width, width), F32), vmem((width, width), F32),
                vmem((planes - 1, 2, 2 * share, width), F32),
                vmem((2, 2, share, width), F32), vmem((2, share, width), F32),
                dma((6,)), dma((6,)), dma((6,)), dma((6,)), dma((6,)), dma((5,)), dma((planes - 1,)), dma((planes - 1,)),
            ],
            compiler_params=pltpu.CompilerParams(collective_id=0, has_side_effects=True, vmem_limit_bytes=40 * 2**20),
        )(mode_shapes.reshape(2, rows, width), mass_blocks, block_cols, send_lists)

    return jax.shard_map(
        local,
        mesh=mesh,
        in_specs=(
            P("sweep", None, "dof", None),
            P(None, None, None, "dof"),
            P(None, "dof"),
            P("dof", None, None),
        ),
        out_specs=P("dof", "sweep", None),
        check_vma=False,
    )
```

```python
import jax
import jax.numpy as jnp
from jax import lax
from jax.experimental import pallas as pl
from jax.experimental.pallas import tpu as pltpu
from jax.sharding import PartitionSpec as P

MESH = pl.DeviceIdType.MESH
F32, BF16 = jnp.float32, jnp.bfloat16
HALVES = 2
GROUP = 2
PARTS = 6
WINDOW = 4
C_PARTS = 6
C_FROM = 0
CUT = 8
PACK = 1024
LISTS = 384


def dot(a, b):
    return jnp.dot(a, b, preferred_element_type=F32)


def dot_t(a, b):
    return lax.dot_general(a, b, (((0,), (0,)), ((), ())), preferred_element_type=F32)


def margins_kernel(n_sweep, n_dof, modes_in, mass_in, cols_in, lists_in, out, modes, mass, cols, lists, fq, fr, cb, mass_own, cols_own, pk_own, pk_q, pk_r, cols_q, cols_r,
                   mt_hi, mt_lo, mq_hi, mq_lo, mr_hi, mr_lo, ya_own, ya_halo, yb, g_q, g_r, cs_q, cs_r, part, acc_bt, rsb, tot,
                   last, z_ss, z_rs, x_ss, x_rs, c_ss, c_rs, m_ss, m_rs, e_ss, e_rs, a_ss, a_rs, b_ss, b_rs, in_s):
    nodes, halo, width = cols.shape[1], lists.shape[2], modes.shape[2]
    rows = 3 * nodes
    planes = n_dof // 2
    half = width // HALVES
    w, p = lax.axis_index("sweep"), lax.axis_index("dof")
    k, z_hi = p // 2, lax.rem(p, 2)
    far = {"dof": 2 * k + (1 - z_hi)}
    seat = lax.rem(w, GROUP)

    def plane(kk):
        return {"dof": 2 * lax.rem(kk + planes, planes) + z_hi}

    def sweep_step(by):
        return {"sweep": lax.rem(w + by + n_sweep, n_sweep)}

    def groupmate(t):
        return {"sweep": w - seat + lax.rem(seat + t, GROUP)}

    is_last = w == n_sweep - 1

    barrier = pltpu.get_barrier_semaphore()
    greeted = [far, sweep_step(1), sweep_step(-1)]
    greeted += [groupmate(t) for t in range(1, GROUP)]
    greeted += [plane(k + t) for t in range(1, planes)]
    for device in greeted:
        pl.semaphore_signal(barrier, inc=1, device_id=device, device_id_type=MESH)

    loads = [pltpu.make_async_copy(src, dst, in_s.at[i])
             for i, (src, dst) in enumerate(((mass_in, mass), (cols_in, cols), (lists_in, lists), (modes_in, modes)))]
    for load in loads:
        load.start()
    for load in loads[0:3]:
        load.wait()

    def wide(parts):
        filled = sum(part.shape[1] for part in parts)
        return jnp.concatenate(parts + [jnp.zeros((parts[0].shape[0], PACK - filled), F32)], axis=1)

    columns = cols[...].astype(F32)
    own_lists = lists[0].astype(F32)
    cols_own[...] = jnp.concatenate([columns] * 3, axis=1)
    for d in range(3):
        block = [mass[c, d] for c in range(3)]
        mass_own[d] = jnp.concatenate(block, axis=1)
        pk_own[d] = wide(block)
    pk_own[0, 0:1, :] = wide([columns[b:b + 1] for b in (1, 2, 3)])
    pk_own[1, 0:1, :] = wide([columns[b:b + 1] for b in (4, 5, 6)])
    pk_own[2, 0:1, :] = wide([columns[7:8], jnp.zeros((1, LISTS - nodes), F32), own_lists[0:1], own_lists[1:2]])

    pl.semaphore_wait(barrier, len(greeted))

    def remote(src, dst, send, recv, device):
        return pltpu.make_async_remote_copy(src_ref=src, dst_ref=dst, send_sem=send, recv_sem=recv, device_id=device,
                                            device_id_type=MESH)

    chunks = [(c, h) for h in range(HALVES) for c in range(PARTS)]

    def piece(ref, c, h):
        return ref.at[pl.ds(c * (rows // PARTS), rows // PARTS), pl.ds(h * half, half)]

    def strip(ref, c):
        return ref.at[pl.ds(c * (rows // C_PARTS), rows // C_PARTS)]

    x_next = plane(k + 1 - 2 * z_hi)
    mine = pl.ds(pl.multiple_of(seat * (PACK // GROUP), PACK // GROUP), PACK // GROUP)
    z_copies = [remote(piece(modes_in.at[1], c, h), piece(fq, c, h), z_ss.at[i], z_rs.at[i], far) for i, (c, h) in enumerate(chunks)]
    x_copies = [remote(piece(fq, c, h), piece(fr, c, h), x_ss.at[i], x_rs.at[i], x_next) for i, (c, h) in enumerate(chunks)]
    c_copies = [remote(strip(modes_in.at[0], i), strip(cb, i), c_ss.at[i], c_rs.at[i], sweep_step(-1)) for i in range(C_PARTS)]
    own_copy = remote(pk_own.at[:, :, mine], pk_q.at[:, :, mine], m_ss.at[1], m_rs.at[1], far)
    e_copies = [remote(pk_q.at[:, :, mine], pk_q.at[:, :, mine], e_ss.at[t - 1], e_rs.at[t - 1], groupmate(t)) for t in range(1, GROUP)]
    pack_copy = remote(pk_q, pk_r, m_ss.at[2], m_rs.at[2], x_next)

    def pump(i):
        z_copies[i].wait_recv()
        x_copies[i].start()
        if i + WINDOW < len(chunks):
            z_copies[i + WINDOW].start()
        if C_FROM <= i < C_FROM + C_PARTS:
            @pl.when(w > 0)
            def _():
                c_copies[i - C_FROM].start()

    own_copy.start()

    @pl.when(w // 2 < CUT)
    def _():
        for i in range(WINDOW):
            z_copies[i].start()

    def build(masses, columns, slots, offset, begin, count, hi, lo):
        def body(g, carry):
            r = pl.multiple_of(g * 16, 16)
            for lane, lanes in ((0, 512), (512, rows - 512)):
                ids = (lax.broadcasted_iota(jnp.int32, (16, lanes), 0) + (r + offset)).astype(F32)
                sums = [jnp.zeros((16, lanes), F32) for _ in range(3)]
                for b in slots:
                    hit = ids == columns[b:b + 1, lane:lane + lanes]
                    for d in range(3):
                        sums[d] = sums[d] + jnp.where(hit, masses[d, b:b + 1, lane:lane + lanes], 0.0)
                for d in range(3):
                    top = sums[d].astype(BF16)
                    hi[d, pl.ds(r, 16), lane:lane + lanes] = top
                    lo[d, pl.ds(r, 16), lane:lane + lanes] = (sums[d] - top.astype(F32)).astype(BF16)
            return carry

        lax.fori_loop(begin // 16, count // 16, body, 0)

    def one_hot(row):
        ids = lax.broadcasted_iota(jnp.int32, (nodes, halo), 0).astype(F32)
        return jnp.where(ids == row, 1.0, 0.0).astype(BF16)

    def side_rows(pk, columns, seg_here, row_there, seg_there, hi, lo, g):
        for b in range(1, 8):
            at = (b - 1) % 3 * nodes
            columns[b:b + 1, :] = jnp.concatenate([pk[(b - 1) // 3, 0:1, at:at + nodes]] * 3, axis=1)
        there = one_hot(jnp.where(row_there == 0, pk[2, 0:1, LISTS:LISTS + halo], pk[2, 0:1, LISTS + halo:LISTS + 2 * halo]))
        build(pk, columns, range(1, 8), nodes + halo * seg_there, 0, halo, hi, lo)
        spread = [dot(there, ya_halo[d, pl.ds(pl.multiple_of(halo * seg_here, halo), halo), :]).T for d in range(3)]
        g[...] = jnp.concatenate(spread, axis=1).astype(BF16)

    def side_partner(row_here, cs):
        here = one_hot(jnp.where(row_here == 0, lists[0, 0:1, :], lists[0, 1:2, :]).astype(F32))
        for d in range(3):
            cs[:, d * halo:(d + 1) * halo] = dot_t(cb[pl.ds(d * nodes, nodes), :], here).astype(BF16)

    def use_first(field, g, h):
        lanes = slice(h * half, (h + 1) * half)
        part[0, :, lanes] += dot(g[...], field[:, lanes])

    def use_second(field, hi, lo, cs, h):
        lanes = slice(h * half, (h + 1) * half)
        block = field[:, lanes]
        y = (dot(hi[...].reshape(3 * halo, rows), block) + dot(lo[...].reshape(3 * halo, rows), block)).astype(BF16)
        acc_bt[:, lanes] += dot(cs[...], y)

    ext = nodes + 2 * halo
    build(mass_own, cols_own, range(8), 0, 0, ext // 2, mt_hi, mt_lo)
    own_copy.wait_recv()
    for copy in e_copies:
        copy.start()
    build(mass_own, cols_own, range(8), 0, ext // 2, ext, mt_hi, mt_lo)

    @pl.when(w // 2 >= CUT)
    def _():
        for i in range(WINDOW):
            z_copies[i].start()

    for copy in e_copies:
        copy.wait_recv()
    pack_copy.start()
    loads[3].wait()

    for d in range(3):
        pump(d)
        first = dot(mt_hi[d], modes[0]) + dot(mt_lo[d], modes[0])
        ya_own[pl.ds(d * nodes, nodes), :] = first[0:nodes].astype(BF16)
        ya_halo[d] = first[nodes:].astype(BF16)
    pump(3)
    part[0] = dot_t(ya_own[...], modes[1])
    for d in range(3):
        second = dot(mt_hi[d, 0:nodes], modes[1]) + dot(mt_lo[d, 0:nodes], modes[1])
        yb[pl.ds(d * nodes, nodes), :] = second.astype(BF16)
    pump(4)
    side_rows(pk_q, cols_q, 1 - z_hi, 1 - z_hi, z_hi, mq_hi, mq_lo, g_q)
    pump(5)
    pack_copy.wait_recv()
    side_rows(pk_r, cols_r, z_hi, z_hi, 1 - z_hi, mr_hi, mr_lo, g_r)
    pump(6)
    use_first(fq, g_q, 0)
    pump(7)

    @pl.when(jnp.logical_not(is_last))
    def _():
        for copy in c_copies:
            copy.wait_recv()

    @pl.when(is_last)
    def _():
        cb[...] = modes[1]

    acc_bt[...] = dot_t(cb[...], yb[...])
    side_partner(z_hi, cs_q)
    side_partner(1 - z_hi, cs_r)
    use_second(fq, mq_hi, mq_lo, cs_q, 0)
    pump(8)

    share = width // n_dof
    pair = 2 * share
    a_copies, b_copies = [], []
    for h in range(HALVES):
        for t in range(1, planes):
            there = pl.ds(pl.multiple_of(lax.rem(k + t, planes) * pair, pair), pair)
            lanes = pl.ds(h * half, half)
            a_copies.append(remote(part.at[0, there, lanes], rsb.at[t - 1, 0, :, lanes], a_ss.at[h, t - 1], a_rs.at[h, t - 1],
                                   plane(k + t)))
            if h == 0:
                b_copies.append(remote(part.at[1, there], rsb.at[t - 1, 1], b_ss.at[t - 1], b_rs.at[t - 1], plane(k + t)))

    for h in range(HALVES):
        lanes = slice(h * half, (h + 1) * half)
        if h > 0:
            for i in range(9, h * PARTS + PARTS):
                pump(i)
            use_first(fq, g_q, h)
            use_second(fq, mq_hi, mq_lo, cs_q, h)
        for i in range(h * PARTS, h * PARTS + PARTS):
            x_copies[i].wait_recv()
        use_first(fr, g_r, h)
        for t in range(1, planes):
            a_copies[h * (planes - 1) + t - 1].start()
        use_second(fr, mr_hi, mr_lo, cs_r, h)
        part[1, lanes, :] = acc_bt[:, lanes].T
        for t in range(1, planes):
            @pl.when(lax.rem(k + t, planes) // (planes // HALVES) == h)
            def _():
                b_copies[t - 1].start()

    total = part[:, pl.ds(pl.multiple_of(k * pair, pair), pair), :]
    for t in range(1, planes):
        for h in range(HALVES):
            a_copies[h * (planes - 1) + t - 1].wait_recv()
        b_copies[t - 1].wait_recv()
        total = total + rsb[t - 1]
    tot[:, 0] = total[:, 0:share]
    tot[:, 1] = total[:, share:]
    last_copy = remote(tot.at[:, 1 - z_hi], last, m_ss.at[3], m_rs.at[3], far)
    last_copy.start()

    for copy in z_copies + x_copies + a_copies + b_copies + e_copies:
        copy.wait_send()

    @pl.when(w > 0)
    def _():
        for copy in c_copies:
            copy.wait_send()

    own_copy.wait_send()
    pack_copy.wait_send()
    last_copy.wait()
    for s in range(2):
        out[:, s, :] = tot[s, pl.ds(z_hi, 1)][0] + last[s]


def solution(mesh):
    n_sweep, n_dof = mesh.shape["sweep"], mesh.shape["dof"]

    def local(mode_shapes, mass_blocks, block_cols, send_lists):
        _, _, nodes, width = mode_shapes.shape
        halo = send_lists.shape[2]
        rows, planes, share = 3 * nodes, n_dof // 2, width // n_dof
        ext = nodes + 2 * halo
        vmem = pltpu.VMEM
        dma = pltpu.SemaphoreType.DMA
        return pl.pallas_call(
            lambda *refs: margins_kernel(n_sweep, n_dof, *refs),
            out_shape=jax.ShapeDtypeStruct((share, 2, width), F32),
            in_specs=[pl.BlockSpec(memory_space=pltpu.HBM)] * 4,
            out_specs=pl.BlockSpec(memory_space=pltpu.VMEM),
            scratch_shapes=[
                vmem((2, rows, width), BF16), vmem(mass_blocks.shape, F32), vmem(block_cols.shape, jnp.int32), vmem(send_lists.shape, jnp.int32),
                vmem((rows, width), BF16), vmem((rows, width), BF16), vmem((rows, width), BF16),
                vmem((3, 8, rows), F32), vmem((8, rows), F32),
                vmem((3, 8, PACK), F32), vmem((3, 8, PACK), F32), vmem((3, 8, PACK), F32), vmem((8, rows), F32), vmem((8, rows), F32),
                vmem((3, ext, rows), BF16), vmem((3, ext, rows), BF16),
                vmem((3, halo, rows), BF16), vmem((3, halo, rows), BF16),
                vmem((3, halo, rows), BF16), vmem((3, halo, rows), BF16),
                vmem((rows, width), BF16), vmem((3, 2 * halo, width), BF16), vmem((rows, width), BF16),
                vmem((width, rows), BF16), vmem((width, rows), BF16),
                vmem((width, 3 * halo), BF16), vmem((width, 3 * halo), BF16),
                vmem((2, width, width), F32), vmem((width, width), F32),
                vmem((planes - 1, 2, 2 * share, width), F32),
                vmem((2, 2, share, width), F32), vmem((2, share, width), F32),
                dma((HALVES * PARTS,)), dma((HALVES * PARTS,)), dma((HALVES * PARTS,)), dma((HALVES * PARTS,)),
                dma((C_PARTS,)), dma((C_PARTS,)), dma((4,)), dma((4,)), dma((GROUP - 1,)), dma((GROUP - 1,)),
                dma((HALVES, planes - 1)), dma((HALVES, planes - 1)), dma((planes - 1,)), dma((planes - 1,)), dma((4,)),
            ],
            compiler_params=pltpu.CompilerParams(collective_id=0, has_side_effects=True, vmem_limit_bytes=40 * 2**20),
        )(mode_shapes.reshape(2, rows, width), mass_blocks, block_cols, send_lists)

    return jax.shard_map(
        local,
        mesh=mesh,
        in_specs=(
            P("sweep", None, "dof", None),
            P(None, None, None, "dof"),
            P(None, "dof"),
            P("dof", None, None),
        ),
        out_specs=P("dof", "sweep", None),
        check_vma=False,
    )
```

```python
import jax
import jax.numpy as jnp
from jax import lax
from jax.experimental import pallas as pl
from jax.experimental.pallas import tpu as pltpu
from jax.sharding import PartitionSpec as P

MESH = pl.DeviceIdType.MESH
F32, BF16 = jnp.float32, jnp.bfloat16
HALVES = 2
GROUP = 2
PARTS = 6
FIRST = 1
WINDOW = 4
CUT = 4
C_PARTS = 6
E_SOON = 1
PACK = 1024
LISTS = 384


def dot(a, b):
    return jnp.dot(a, b, preferred_element_type=F32)


def dot_t(a, b):
    return lax.dot_general(a, b, (((0,), (0,)), ((), ())), preferred_element_type=F32)


def margins_kernel(n_sweep, n_dof, modes_in, mass_in, cols_in, lists_in, out, modes, mass, cols, lists, fq, fr, cb, relay, mass_own, cols_own, pk_own, pk_q, pk_r, cols_q, cols_r,
                   mt_hi, mt_lo, mq_hi, mq_lo, mr_hi, mr_lo, ya_own, ya_halo, yb, g_q, g_r, cs_q, cs_r, part, acc_bt, rsb, tot,
                   last, z_ss, z_rs, x_ss, x_rs, c_ss, c_rs, ri_ss, ri_rs, ro_ss, m_ss, m_rs, e_ss, e_rs, a_ss, a_rs, b_ss, b_rs, in_s):
    nodes, halo, width = cols.shape[1], lists.shape[2], modes.shape[2]
    rows = 3 * nodes
    planes = n_dof // 2
    half = width // HALVES
    w, p = lax.axis_index("sweep"), lax.axis_index("dof")
    k, z_hi = p // 2, lax.rem(p, 2)
    far = {"dof": 2 * k + (1 - z_hi)}
    seat = lax.rem(w, GROUP)

    def plane(kk):
        return {"dof": 2 * lax.rem(kk + planes, planes) + z_hi}

    def sweep_step(by):
        return {"sweep": lax.rem(w + by + n_sweep, n_sweep)}

    def groupmate(t):
        return {"sweep": w - seat + lax.rem(seat + t, GROUP)}

    is_last = w == n_sweep - 1

    barrier = pltpu.get_barrier_semaphore()
    greeted = [far]
    greeted += [groupmate(t) for t in range(1, GROUP)]
    greeted += [plane(k + t) for t in range(1, planes)]
    for device in greeted:
        pl.semaphore_signal(barrier, inc=1, device_id=device, device_id_type=MESH)

    @pl.when(w > 0)
    def _():
        pl.semaphore_signal(barrier, inc=1, device_id=sweep_step(-1), device_id_type=MESH)

    @pl.when(w > 1)
    def _():
        pl.semaphore_signal(barrier, inc=1, device_id=sweep_step(-2), device_id_type=MESH)

    @pl.when(jnp.logical_not(is_last))
    def _():
        pl.semaphore_signal(barrier, inc=1, device_id=sweep_step(1), device_id_type=MESH)

    @pl.when(w < n_sweep - 2)
    def _():
        pl.semaphore_signal(barrier, inc=1, device_id=sweep_step(2), device_id_type=MESH)

    loads = [pltpu.make_async_copy(src, dst, in_s.at[i])
             for i, (src, dst) in enumerate(((mass_in, mass), (cols_in, cols), (lists_in, lists), (modes_in, modes)))]
    for load in loads:
        load.start()
    beside = [w > 0, w > 1, w < n_sweep - 1, w < n_sweep - 2]
    pl.semaphore_wait(barrier, len(greeted) + sum(jnp.where(near, 1, 0) for near in beside))

    def remote(src, dst, send, recv, device):
        return pltpu.make_async_remote_copy(src_ref=src, dst_ref=dst, send_sem=send, recv_sem=recv, device_id=device,
                                            device_id_type=MESH)

    chunks = [(c, h) for h in range(HALVES) for c in range(PARTS)]

    def piece(ref, c, h):
        return ref.at[pl.ds(c * (rows // PARTS), rows // PARTS), pl.ds(h * half, half)]

    def strip(ref, c):
        return ref.at[pl.ds(c * (rows // C_PARTS), rows // C_PARTS)]

    x_next = plane(k + 1 - 2 * z_hi)
    mine = pl.ds(pl.multiple_of(seat * (PACK // GROUP), PACK // GROUP), PACK // GROUP)
    z_copies = [remote(piece(modes_in.at[1], c, h), piece(fq, c, h), z_ss.at[i], z_rs.at[i], far) for i, (c, h) in enumerate(chunks)]
    x_copies = [remote(piece(fq, c, h), piece(fr, c, h), x_ss.at[i], x_rs.at[i], x_next) for i, (c, h) in enumerate(chunks)]
    c_copies = [remote(strip(modes_in.at[0], i), strip(cb, i), c_ss.at[i], c_rs.at[i], sweep_step(-1)) for i in range(C_PARTS)]
    c_split = C_PARTS // 2
    in_copies = [remote(strip(modes_in.at[0], i), strip(relay, i - c_split), ri_ss.at[i - c_split], ri_rs.at[i - c_split], sweep_step(1))
                 for i in range(c_split, C_PARTS)]
    out_copies = [remote(strip(relay, i - c_split), strip(cb, i), ro_ss.at[i - c_split], c_rs.at[i], sweep_step(-2))
                  for i in range(c_split, C_PARTS)]
    core = lax.rem(w, 2)
    own_copy = remote(pk_own.at[:, :, mine], pk_q.at[:, :, mine], m_ss.at[1], m_rs.at[1], far)
    e_copies = [remote(pk_q.at[:, :, mine], pk_q.at[:, :, mine], e_ss.at[t - 1], e_rs.at[t - 1], groupmate(t)) for t in range(1, GROUP)]
    pack_copy = remote(pk_q, pk_r, m_ss.at[2], m_rs.at[2], x_next)

    pumped = [0]

    def pump(twelfths):
        upto = len(chunks) * twelfths // 12
        for i in range(pumped[0], upto):
            z_copies[i].wait_recv()
            x_copies[i].start()
            if i + WINDOW < len(chunks):
                @pl.when(w // 2 >= CUT)
                def _():
                    z_copies[i + WINDOW].start()
        pumped[0] = upto

    @pl.when(jnp.logical_and(core == 0, w > 0))
    def _():
        for copy in in_copies:
            copy.start()

    for i in range(FIRST):
        z_copies[i].start()

    for load in loads[0:3]:
        load.wait()

    def wide(parts):
        filled = sum(part.shape[1] for part in parts)
        return jnp.concatenate(parts + [jnp.zeros((parts[0].shape[0], PACK - filled), F32)], axis=1)

    columns = cols[...].astype(F32)
    own_lists = lists[0].astype(F32)
    cols_own[...] = jnp.concatenate([columns] * 3, axis=1)
    for d in range(3):
        block = [mass[c, d] for c in range(3)]
        mass_own[d] = jnp.concatenate(block, axis=1)
        pk_own[d] = wide(block)
    pk_own[0, 0:1, :] = wide([columns[b:b + 1] for b in (1, 2, 3)])
    pk_own[1, 0:1, :] = wide([columns[b:b + 1] for b in (4, 5, 6)])
    pk_own[2, 0:1, :] = wide([columns[7:8], jnp.zeros((1, LISTS - nodes), F32), own_lists[0:1], own_lists[1:2]])

    own_copy.start()
    for i in range(FIRST, WINDOW):
        z_copies[i].start()

    @pl.when(w > 0)
    def _():
        for copy in c_copies[:c_split]:
            copy.start()

    @pl.when(core == 1)
    def _():
        for copy in c_copies[c_split:]:
            copy.start()

    @pl.when(w // 2 < CUT)
    def _():
        for copy in z_copies[WINDOW:]:
            copy.start()

    def build(masses, columns, slots, offset, begin, count, hi, lo):
        def body(g, carry):
            r = pl.multiple_of(g * 16, 16)
            for lane, lanes in ((0, 512), (512, rows - 512)):
                ids = (lax.broadcasted_iota(jnp.int32, (16, lanes), 0) + (r + offset)).astype(F32)
                sums = [jnp.zeros((16, lanes), F32) for _ in range(3)]
                for b in slots:
                    hit = ids == columns[b:b + 1, lane:lane + lanes]
                    for d in range(3):
                        sums[d] = sums[d] + jnp.where(hit, masses[d, b:b + 1, lane:lane + lanes], 0.0)
                for d in range(3):
                    top = sums[d].astype(BF16)
                    hi[d, pl.ds(r, 16), lane:lane + lanes] = top
                    lo[d, pl.ds(r, 16), lane:lane + lanes] = (sums[d] - top.astype(F32)).astype(BF16)
            return carry

        lax.fori_loop(begin // 16, count // 16, body, 0)

    def one_hot(row):
        ids = lax.broadcasted_iota(jnp.int32, (nodes, halo), 0).astype(F32)
        return jnp.where(ids == row, 1.0, 0.0).astype(BF16)

    def side_rows(pk, columns, seg_here, row_there, seg_there, hi, lo, g):
        for b in range(1, 8):
            at = (b - 1) % 3 * nodes
            columns[b:b + 1, :] = jnp.concatenate([pk[(b - 1) // 3, 0:1, at:at + nodes]] * 3, axis=1)
        there = one_hot(jnp.where(row_there == 0, pk[2, 0:1, LISTS:LISTS + halo], pk[2, 0:1, LISTS + halo:LISTS + 2 * halo]))
        build(pk, columns, range(1, 8), nodes + halo * seg_there, 0, halo, hi, lo)
        spread = [dot(there, ya_halo[d, pl.ds(pl.multiple_of(halo * seg_here, halo), halo), :]).T for d in range(3)]
        g[...] = jnp.concatenate(spread, axis=1).astype(BF16)

    def side_partner(row_here, cs):
        here = one_hot(jnp.where(row_here == 0, lists[0, 0:1, :], lists[0, 1:2, :]).astype(F32))
        for d in range(3):
            cs[:, d * halo:(d + 1) * halo] = dot_t(cb[pl.ds(d * nodes, nodes), :], here).astype(BF16)

    def use_first(field, g, h):
        lanes = slice(h * half, (h + 1) * half)
        part[0, :, lanes] += dot(g[...], field[:, lanes])

    def use_second(field, hi, lo, cs, h):
        lanes = slice(h * half, (h + 1) * half)
        block = field[:, lanes]
        y = (dot(hi[...].reshape(3 * halo, rows), block) + dot(lo[...].reshape(3 * halo, rows), block)).astype(BF16)
        acc_bt[:, lanes] += dot(cs[...], y)

    ext = nodes + 2 * halo
    build(mass_own, cols_own, range(8), 0, 0, ext // 2, mt_hi, mt_lo)
    own_copy.wait_recv()
    for copy in e_copies:
        copy.start()

    @pl.when(jnp.logical_and(core == 1, w > 1))
    def _():
        for arrived, copy in zip(in_copies, out_copies):
            arrived.wait_recv()
            copy.start()

    build(mass_own, cols_own, range(8), 0, ext // 2, ext, mt_hi, mt_lo)
    loads[3].wait()
    for d in range(3):
        first = dot(mt_hi[d], modes[0]) + dot(mt_lo[d], modes[0])
        ya_own[pl.ds(d * nodes, nodes), :] = first[0:nodes].astype(BF16)
        ya_halo[d] = first[nodes:].astype(BF16)
        pump(d + 1)
    for copy in e_copies[:E_SOON * len(e_copies)]:
        copy.wait_recv()
    if E_SOON:
        pack_copy.start()
    part[0] = dot_t(ya_own[...], modes[1])
    pump(4)
    for d in range(3):
        second = dot(mt_hi[d, 0:nodes], modes[1]) + dot(mt_lo[d, 0:nodes], modes[1])
        yb[pl.ds(d * nodes, nodes), :] = second.astype(BF16)
    pump(5)
    if not E_SOON:
        for copy in e_copies:
            copy.wait_recv()
        pack_copy.start()
    side_rows(pk_q, cols_q, 1 - z_hi, 1 - z_hi, z_hi, mq_hi, mq_lo, g_q)
    pump(6)
    use_first(fq, g_q, 0)
    pump(7)

    @pl.when(jnp.logical_not(is_last))
    def _():
        for copy in c_copies:
            copy.wait_recv()

    @pl.when(is_last)
    def _():
        cb[...] = modes[1]

    acc_bt[...] = dot_t(cb[...], yb[...])
    side_partner(z_hi, cs_q)
    side_partner(1 - z_hi, cs_r)
    pump(8)
    use_second(fq, mq_hi, mq_lo, cs_q, 0)
    pack_copy.wait_recv()
    side_rows(pk_r, cols_r, z_hi, z_hi, 1 - z_hi, mr_hi, mr_lo, g_r)
    pump(9)

    share = width // n_dof
    pair = 2 * share
    a_copies, b_copies = [], []
    for h in range(HALVES):
        for t in range(1, planes):
            there = pl.ds(pl.multiple_of(lax.rem(k + t, planes) * pair, pair), pair)
            lanes = pl.ds(h * half, half)
            a_copies.append(remote(part.at[0, there, lanes], rsb.at[t - 1, 0, :, lanes], a_ss.at[h, t - 1], a_rs.at[h, t - 1],
                                   plane(k + t)))
            if h == 0:
                b_copies.append(remote(part.at[1, there], rsb.at[t - 1, 1], b_ss.at[t - 1], b_rs.at[t - 1], plane(k + t)))

    for h in range(HALVES):
        lanes = slice(h * half, (h + 1) * half)
        if h > 0:
            pump(12)
            use_first(fq, g_q, h)
            use_second(fq, mq_hi, mq_lo, cs_q, h)
        for i in range(h * PARTS, h * PARTS + PARTS):
            x_copies[i].wait_recv()
        use_first(fr, g_r, h)
        for t in range(1, planes):
            a_copies[h * (planes - 1) + t - 1].start()
        use_second(fr, mr_hi, mr_lo, cs_r, h)
        part[1, lanes, :] = acc_bt[:, lanes].T
        for t in range(1, planes):
            @pl.when(lax.rem(k + t, planes) // (planes // HALVES) == h)
            def _():
                b_copies[t - 1].start()

    total = part[:, pl.ds(pl.multiple_of(k * pair, pair), pair), :]
    for t in range(1, planes):
        for h in range(HALVES):
            a_copies[h * (planes - 1) + t - 1].wait_recv()
        b_copies[t - 1].wait_recv()
        total = total + rsb[t - 1]
    tot[:, 0] = total[:, 0:share]
    tot[:, 1] = total[:, share:]
    last_copy = remote(tot.at[:, 1 - z_hi], last, m_ss.at[3], m_rs.at[3], far)
    last_copy.start()

    for copy in z_copies + x_copies + a_copies + b_copies + e_copies:
        copy.wait_send()

    @pl.when(w > 0)
    def _():
        for copy in c_copies[:c_split]:
            copy.wait_send()

    @pl.when(core == 1)
    def _():
        for copy in c_copies[c_split:]:
            copy.wait_send()

    @pl.when(jnp.logical_and(core == 1, w > 1))
    def _():
        for copy in out_copies:
            copy.wait_send()

    @pl.when(jnp.logical_and(core == 0, w > 0))
    def _():
        for copy in in_copies:
            copy.wait_send()

    own_copy.wait_send()
    pack_copy.wait_send()
    last_copy.wait()
    for s in range(2):
        out[:, s, :] = tot[s, pl.ds(z_hi, 1)][0] + last[s]


def solution(mesh):
    n_sweep, n_dof = mesh.shape["sweep"], mesh.shape["dof"]

    def local(mode_shapes, mass_blocks, block_cols, send_lists):
        _, _, nodes, width = mode_shapes.shape
        halo = send_lists.shape[2]
        rows, planes, share = 3 * nodes, n_dof // 2, width // n_dof
        ext = nodes + 2 * halo
        vmem = pltpu.VMEM
        dma = pltpu.SemaphoreType.DMA
        return pl.pallas_call(
            lambda *refs: margins_kernel(n_sweep, n_dof, *refs),
            out_shape=jax.ShapeDtypeStruct((share, 2, width), F32),
            in_specs=[pl.BlockSpec(memory_space=pltpu.HBM)] * 4,
            out_specs=pl.BlockSpec(memory_space=pltpu.VMEM),
            scratch_shapes=[
                vmem((2, rows, width), BF16), vmem(mass_blocks.shape, F32), vmem(block_cols.shape, jnp.int32), vmem(send_lists.shape, jnp.int32),
                vmem((rows, width), BF16), vmem((rows, width), BF16), vmem((rows, width), BF16),
                vmem((rows // 2, width), BF16),
                vmem((3, 8, rows), F32), vmem((8, rows), F32),
                vmem((3, 8, PACK), F32), vmem((3, 8, PACK), F32), vmem((3, 8, PACK), F32), vmem((8, rows), F32), vmem((8, rows), F32),
                vmem((3, ext, rows), BF16), vmem((3, ext, rows), BF16),
                vmem((3, halo, rows), BF16), vmem((3, halo, rows), BF16),
                vmem((3, halo, rows), BF16), vmem((3, halo, rows), BF16),
                vmem((rows, width), BF16), vmem((3, 2 * halo, width), BF16), vmem((rows, width), BF16),
                vmem((width, rows), BF16), vmem((width, rows), BF16),
                vmem((width, 3 * halo), BF16), vmem((width, 3 * halo), BF16),
                vmem((2, width, width), F32), vmem((width, width), F32),
                vmem((planes - 1, 2, 2 * share, width), F32),
                vmem((2, 2, share, width), F32), vmem((2, share, width), F32),
                dma((HALVES * PARTS,)), dma((HALVES * PARTS,)), dma((HALVES * PARTS,)), dma((HALVES * PARTS,)),
                dma((C_PARTS,)), dma((C_PARTS,)), dma((C_PARTS // 2,)), dma((C_PARTS // 2,)), dma((C_PARTS // 2,)), dma((4,)), dma((4,)), dma((GROUP - 1,)), dma((GROUP - 1,)),
                dma((HALVES, planes - 1)), dma((HALVES, planes - 1)), dma((planes - 1,)), dma((planes - 1,)), dma((4,)),
            ],
            compiler_params=pltpu.CompilerParams(collective_id=0, has_side_effects=True, vmem_limit_bytes=40 * 2**20),
        )(mode_shapes.reshape(2, rows, width), mass_blocks, block_cols, send_lists)

    return jax.shard_map(
        local,
        mesh=mesh,
        in_specs=(
            P("sweep", None, "dof", None),
            P(None, None, None, "dof"),
            P(None, "dof"),
            P("dof", None, None),
        ),
        out_specs=P("dof", "sweep", None),
        check_vma=False,
    )
```

```python
import jax
import jax.numpy as jnp
from jax import lax
from jax.experimental import pallas as pl
from jax.experimental.pallas import tpu as pltpu
from jax.sharding import PartitionSpec as P

MESH = pl.DeviceIdType.MESH
F32, BF16 = jnp.float32, jnp.bfloat16
HALVES = 2
GROUP = 2
PARTS = 6
FIRST = 1
WINDOW = 4
DEPTH = 768
CUT = 4
C_PARTS = 6
E_SOON = 1
PACK = 1024
LISTS = 384


def dot(a, b):
    return jnp.dot(a, b, preferred_element_type=F32)


def dot_t(a, b):
    return lax.dot_general(a, b, (((0,), (0,)), ((), ())), preferred_element_type=F32)


def margins_kernel(n_sweep, n_dof, modes_in, mass_in, cols_in, lists_in, out, modes, mass, cols, lists, fq, fr, cb, relay, mass_own, cols_own, pk_own, pk_q, pk_r, cols_q, cols_r,
                   mt_hi, mt_lo, mq_hi, mq_lo, mr_hi, mr_lo, ya_own, ya_halo, yb, g_q, g_r, cs_q, cs_r, part, acc_bt, rsb, tot,
                   last, z_ss, z_rs, x_ss, x_rs, c_ss, c_rs, ri_ss, ri_rs, ro_ss, m_ss, m_rs, e_ss, e_rs, a_ss, a_rs, b_ss, b_rs, in_s):
    nodes, halo, width = cols.shape[1], lists.shape[2], modes.shape[2]
    rows = 3 * nodes
    planes = n_dof // 2
    half = width // HALVES
    w, p = lax.axis_index("sweep"), lax.axis_index("dof")
    k, z_hi = p // 2, lax.rem(p, 2)
    far = {"dof": 2 * k + (1 - z_hi)}
    seat = lax.rem(w, GROUP)

    def plane(kk):
        return {"dof": 2 * lax.rem(kk + planes, planes) + z_hi}

    def sweep_step(by):
        return {"sweep": lax.rem(w + by + n_sweep, n_sweep)}

    def groupmate(t):
        return {"sweep": w - seat + lax.rem(seat + t, GROUP)}

    is_last = w == n_sweep - 1

    barrier = pltpu.get_barrier_semaphore()
    greeted = [far]
    greeted += [groupmate(t) for t in range(1, GROUP)]
    greeted += [plane(k + t) for t in range(1, planes)]
    for device in greeted:
        pl.semaphore_signal(barrier, inc=1, device_id=device, device_id_type=MESH)

    @pl.when(w > 0)
    def _():
        pl.semaphore_signal(barrier, inc=1, device_id=sweep_step(-1), device_id_type=MESH)

    @pl.when(w > 1)
    def _():
        pl.semaphore_signal(barrier, inc=1, device_id=sweep_step(-2), device_id_type=MESH)

    @pl.when(jnp.logical_not(is_last))
    def _():
        pl.semaphore_signal(barrier, inc=1, device_id=sweep_step(1), device_id_type=MESH)

    @pl.when(w < n_sweep - 2)
    def _():
        pl.semaphore_signal(barrier, inc=1, device_id=sweep_step(2), device_id_type=MESH)

    loads = [pltpu.make_async_copy(src, dst, in_s.at[i])
             for i, (src, dst) in enumerate(((mass_in, mass), (cols_in, cols), (lists_in, lists), (modes_in, modes)))]
    for load in loads:
        load.start()
    beside = [w > 0, w > 1, w < n_sweep - 1, w < n_sweep - 2]
    pl.semaphore_wait(barrier, len(greeted) + sum(jnp.where(near, 1, 0) for near in beside))

    def remote(src, dst, send, recv, device):
        return pltpu.make_async_remote_copy(src_ref=src, dst_ref=dst, send_sem=send, recv_sem=recv, device_id=device,
                                            device_id_type=MESH)

    chunks = [(c, h) for h in range(HALVES) for c in range(PARTS)]

    def piece(ref, c, h):
        return ref.at[pl.ds(c * (rows // PARTS), rows // PARTS), pl.ds(h * half, half)]

    def strip(ref, c):
        return ref.at[pl.ds(c * (rows // C_PARTS), rows // C_PARTS)]

    x_next = plane(k + 1 - 2 * z_hi)
    mine = pl.ds(pl.multiple_of(seat * (PACK // GROUP), PACK // GROUP), PACK // GROUP)
    z_copies = [remote(piece(modes_in.at[1], c, h), piece(fq, c, h), z_ss.at[i], z_rs.at[i], far) for i, (c, h) in enumerate(chunks)]
    x_copies = [remote(piece(fq, c, h), piece(fr, c, h), x_ss.at[i], x_rs.at[i], x_next) for i, (c, h) in enumerate(chunks)]
    c_copies = [remote(strip(modes_in.at[0], i), strip(cb, i), c_ss.at[i], c_rs.at[i], sweep_step(-1)) for i in range(C_PARTS)]
    c_split = C_PARTS // 2
    in_copies = [remote(strip(modes_in.at[0], i), strip(relay, i - c_split), ri_ss.at[i - c_split], ri_rs.at[i - c_split], sweep_step(1))
                 for i in range(c_split, C_PARTS)]
    out_copies = [remote(strip(relay, i - c_split), strip(cb, i), ro_ss.at[i - c_split], c_rs.at[i], sweep_step(-2))
                  for i in range(c_split, C_PARTS)]
    core = lax.rem(w, 2)
    own_copy = remote(pk_own.at[:, :, mine], pk_q.at[:, :, mine], m_ss.at[1], m_rs.at[1], far)
    e_copies = [remote(pk_q.at[:, :, mine], pk_q.at[:, :, mine], e_ss.at[t - 1], e_rs.at[t - 1], groupmate(t)) for t in range(1, GROUP)]
    pack_copy = remote(pk_q, pk_r, m_ss.at[2], m_rs.at[2], x_next)

    pumped = [0]

    def pump(twelfths):
        upto = len(chunks) * twelfths // 12
        for i in range(pumped[0], upto):
            z_copies[i].wait_recv()
            x_copies[i].start()
            if i + WINDOW < len(chunks):
                @pl.when(w // 2 >= CUT)
                def _():
                    z_copies[i + WINDOW].start()
        pumped[0] = upto

    @pl.when(jnp.logical_and(core == 0, w > 0))
    def _():
        for copy in in_copies:
            copy.start()

    for i in range(FIRST):
        z_copies[i].start()

    for load in loads[0:3]:
        load.wait()

    def wide(parts):
        filled = sum(part.shape[1] for part in parts)
        return jnp.concatenate(parts + [jnp.zeros((parts[0].shape[0], PACK - filled), F32)], axis=1)

    columns = cols[...].astype(F32)
    own_lists = lists[0].astype(F32)
    cols_own[...] = jnp.concatenate([columns] * 3, axis=1)
    for d in range(3):
        block = [mass[c, d] for c in range(3)]
        mass_own[d] = jnp.concatenate(block, axis=1)
        pk_own[d] = wide(block)
    pk_own[0, 0:1, :] = wide([columns[b:b + 1] for b in (1, 2, 3)])
    pk_own[1, 0:1, :] = wide([columns[b:b + 1] for b in (4, 5, 6)])
    pk_own[2, 0:1, :] = wide([columns[7:8], jnp.zeros((1, LISTS - nodes), F32), own_lists[0:1], own_lists[1:2]])

    own_copy.start()
    for i in range(FIRST, WINDOW):
        z_copies[i].start()

    @pl.when(w > 0)
    def _():
        for copy in c_copies[:c_split]:
            copy.start()

    @pl.when(core == 1)
    def _():
        for copy in c_copies[c_split:]:
            copy.start()

    @pl.when(w // 2 < CUT)
    def _():
        for copy in z_copies[WINDOW:]:
            copy.start()

    def build(masses, columns, slots, offset, begin, count, hi, lo):
        def body(g, carry):
            r = pl.multiple_of(g * 16, 16)
            for lane, lanes in ((0, 512), (512, rows - 512)):
                ids = (lax.broadcasted_iota(jnp.int32, (16, lanes), 0) + (r + offset)).astype(F32)
                sums = [jnp.zeros((16, lanes), F32) for _ in range(3)]
                for b in slots:
                    hit = ids == columns[b:b + 1, lane:lane + lanes]
                    for d in range(3):
                        sums[d] = sums[d] + jnp.where(hit, masses[d, b:b + 1, lane:lane + lanes], 0.0)
                for d in range(3):
                    top = sums[d].astype(BF16)
                    hi[d, pl.ds(r, 16), lane:lane + lanes] = top
                    lo[d, pl.ds(r, 16), lane:lane + lanes] = (sums[d] - top.astype(F32)).astype(BF16)
            return carry

        lax.fori_loop(begin // 16, count // 16, body, 0)

    def one_hot(row):
        ids = lax.broadcasted_iota(jnp.int32, (nodes, halo), 0).astype(F32)
        return jnp.where(ids == row, 1.0, 0.0).astype(BF16)

    def side_rows(pk, columns, seg_here, row_there, seg_there, hi, lo, g):
        for b in range(1, 8):
            at = (b - 1) % 3 * nodes
            columns[b:b + 1, :] = jnp.concatenate([pk[(b - 1) // 3, 0:1, at:at + nodes]] * 3, axis=1)
        there = one_hot(jnp.where(row_there == 0, pk[2, 0:1, LISTS:LISTS + halo], pk[2, 0:1, LISTS + halo:LISTS + 2 * halo]))
        build(pk, columns, range(1, 8), nodes + halo * seg_there, 0, halo, hi, lo)
        fanned = [dot(there, ya_halo[d, pl.ds(pl.multiple_of(halo * seg_here, halo), halo), :]).T for d in range(3)]
        g[...] = jnp.concatenate(fanned, axis=1).astype(BF16)

    def side_partner(row_here, cs):
        here = one_hot(jnp.where(row_here == 0, lists[0, 0:1, :], lists[0, 1:2, :]).astype(F32))
        for d in range(3):
            cs[:, d * halo:(d + 1) * halo] = dot_t(cb[pl.ds(d * nodes, nodes), :], here).astype(BF16)

    def use_first(field, g, h, begin, end):
        lanes = slice(h * half, (h + 1) * half)
        part[0, :, lanes] += dot(g[:, begin:end], field[begin:end, lanes])

    def spread(field, hi, lo, h, begin, end):
        block = field[begin:end, h * half:(h + 1) * half]
        both = [ref[:, :, begin:end].reshape(3 * halo, end - begin) for ref in (hi, lo)]
        return dot(both[0], block) + dot(both[1], block)

    def use_second(y, cs, h):
        acc_bt[:, h * half:(h + 1) * half] += dot(cs[...], y.astype(BF16))

    ext = nodes + 2 * halo
    build(mass_own, cols_own, range(8), 0, 0, ext // 2, mt_hi, mt_lo)
    own_copy.wait_recv()
    for copy in e_copies:
        copy.start()

    @pl.when(jnp.logical_and(core == 1, w > 1))
    def _():
        for arrived, copy in zip(in_copies, out_copies):
            arrived.wait_recv()
            copy.start()

    build(mass_own, cols_own, range(8), 0, ext // 2, ext, mt_hi, mt_lo)
    loads[3].wait()
    for d in range(3):
        first = dot(mt_hi[d], modes[0]) + dot(mt_lo[d], modes[0])
        ya_own[pl.ds(d * nodes, nodes), :] = first[0:nodes].astype(BF16)
        ya_halo[d] = first[nodes:].astype(BF16)
        pump(d + 1)
    for copy in e_copies[:E_SOON * len(e_copies)]:
        copy.wait_recv()
    if E_SOON:
        pack_copy.start()
    part[0] = dot_t(ya_own[...], modes[1])
    pump(4)
    for d in range(3):
        second = dot(mt_hi[d, 0:nodes], modes[1]) + dot(mt_lo[d, 0:nodes], modes[1])
        yb[pl.ds(d * nodes, nodes), :] = second.astype(BF16)
    pump(5)
    if not E_SOON:
        for copy in e_copies:
            copy.wait_recv()
        pack_copy.start()
    side_rows(pk_q, cols_q, 1 - z_hi, 1 - z_hi, z_hi, mq_hi, mq_lo, g_q)
    pump(6)
    use_first(fq, g_q, 0, 0, rows)
    pump(7)

    @pl.when(jnp.logical_not(is_last))
    def _():
        for copy in c_copies:
            copy.wait_recv()

    @pl.when(is_last)
    def _():
        cb[...] = modes[1]

    acc_bt[...] = dot_t(cb[...], yb[...])
    side_partner(z_hi, cs_q)
    side_partner(1 - z_hi, cs_r)
    pump(8)
    use_second(spread(fq, mq_hi, mq_lo, 0, 0, rows), cs_q, 0)
    pack_copy.wait_recv()
    side_rows(pk_r, cols_r, z_hi, z_hi, 1 - z_hi, mr_hi, mr_lo, g_r)
    pump(9)

    share = width // n_dof
    pair = 2 * share
    a_copies, b_copies = [], []
    for h in range(HALVES):
        for t in range(1, planes):
            there = pl.ds(pl.multiple_of(lax.rem(k + t, planes) * pair, pair), pair)
            lanes = pl.ds(h * half, half)
            a_copies.append(remote(part.at[0, there, lanes], rsb.at[t - 1, 0, :, lanes], a_ss.at[h, t - 1], a_rs.at[h, t - 1],
                                   plane(k + t)))
            if h == 0:
                b_copies.append(remote(part.at[1, there], rsb.at[t - 1, 1], b_ss.at[t - 1], b_rs.at[t - 1], plane(k + t)))

    for h in range(HALVES):
        lanes = slice(h * half, (h + 1) * half)
        if h > 0:
            pump(12)
            use_first(fq, g_q, h, 0, rows)
            use_second(spread(fq, mq_hi, mq_lo, h, 0, rows), cs_q, h)
        *ahead, final = x_copies[h * PARTS:h * PARTS + PARTS]
        for copy in ahead:
            copy.wait_recv()
        use_first(fr, g_r, h, 0, DEPTH)
        y = spread(fr, mr_hi, mr_lo, h, 0, DEPTH)
        if h > 0:
            for copy in a_copies[:planes - 1]:
                copy.wait_recv()
        final.wait_recv()
        use_first(fr, g_r, h, DEPTH, rows)
        for t in range(1, planes):
            a_copies[h * (planes - 1) + t - 1].start()
        use_second(y + spread(fr, mr_hi, mr_lo, h, DEPTH, rows), cs_r, h)
        part[1, lanes, :] = acc_bt[:, lanes].T
        for t in range(1, planes):
            @pl.when(lax.rem(k + t, planes) // (planes // HALVES) == h)
            def _():
                b_copies[t - 1].start()

    total = part[:, pl.ds(pl.multiple_of(k * pair, pair), pair), :]
    for t in range(1, planes):
        a_copies[planes - 1 + t - 1].wait_recv()
        b_copies[t - 1].wait_recv()
        total = total + rsb[t - 1]
    tot[:, 0] = total[:, 0:share]
    tot[:, 1] = total[:, share:]
    last_copy = remote(tot.at[:, 1 - z_hi], last, m_ss.at[3], m_rs.at[3], far)
    last_copy.start()

    for copy in z_copies + x_copies + a_copies + b_copies + e_copies:
        copy.wait_send()

    @pl.when(w > 0)
    def _():
        for copy in c_copies[:c_split]:
            copy.wait_send()

    @pl.when(core == 1)
    def _():
        for copy in c_copies[c_split:]:
            copy.wait_send()

    @pl.when(jnp.logical_and(core == 1, w > 1))
    def _():
        for copy in out_copies:
            copy.wait_send()

    @pl.when(jnp.logical_and(core == 0, w > 0))
    def _():
        for copy in in_copies:
            copy.wait_send()

    own_copy.wait_send()
    pack_copy.wait_send()
    last_copy.wait()
    for s in range(2):
        out[:, s, :] = tot[s, pl.ds(z_hi, 1)][0] + last[s]


def solution(mesh):
    n_sweep, n_dof = mesh.shape["sweep"], mesh.shape["dof"]

    def local(mode_shapes, mass_blocks, block_cols, send_lists):
        _, _, nodes, width = mode_shapes.shape
        halo = send_lists.shape[2]
        rows, planes, share = 3 * nodes, n_dof // 2, width // n_dof
        ext = nodes + 2 * halo
        vmem = pltpu.VMEM
        dma = pltpu.SemaphoreType.DMA
        return pl.pallas_call(
            lambda *refs: margins_kernel(n_sweep, n_dof, *refs),
            out_shape=jax.ShapeDtypeStruct((share, 2, width), F32),
            in_specs=[pl.BlockSpec(memory_space=pltpu.HBM)] * 4,
            out_specs=pl.BlockSpec(memory_space=pltpu.VMEM),
            scratch_shapes=[
                vmem((2, rows, width), BF16), vmem(mass_blocks.shape, F32), vmem(block_cols.shape, jnp.int32), vmem(send_lists.shape, jnp.int32),
                vmem((rows, width), BF16), vmem((rows, width), BF16), vmem((rows, width), BF16),
                vmem((rows // 2, width), BF16),
                vmem((3, 8, rows), F32), vmem((8, rows), F32),
                vmem((3, 8, PACK), F32), vmem((3, 8, PACK), F32), vmem((3, 8, PACK), F32), vmem((8, rows), F32), vmem((8, rows), F32),
                vmem((3, ext, rows), BF16), vmem((3, ext, rows), BF16),
                vmem((3, halo, rows), BF16), vmem((3, halo, rows), BF16),
                vmem((3, halo, rows), BF16), vmem((3, halo, rows), BF16),
                vmem((rows, width), BF16), vmem((3, 2 * halo, width), BF16), vmem((rows, width), BF16),
                vmem((width, rows), BF16), vmem((width, rows), BF16),
                vmem((width, 3 * halo), BF16), vmem((width, 3 * halo), BF16),
                vmem((2, width, width), F32), vmem((width, width), F32),
                vmem((planes - 1, 2, 2 * share, width), F32),
                vmem((2, 2, share, width), F32), vmem((2, share, width), F32),
                dma((HALVES * PARTS,)), dma((HALVES * PARTS,)), dma((HALVES * PARTS,)), dma((HALVES * PARTS,)),
                dma((C_PARTS,)), dma((C_PARTS,)), dma((C_PARTS // 2,)), dma((C_PARTS // 2,)), dma((C_PARTS // 2,)), dma((4,)), dma((4,)), dma((GROUP - 1,)), dma((GROUP - 1,)),
                dma((HALVES, planes - 1)), dma((HALVES, planes - 1)), dma((planes - 1,)), dma((planes - 1,)), dma((4,)),
            ],
            compiler_params=pltpu.CompilerParams(collective_id=0, has_side_effects=True, vmem_limit_bytes=40 * 2**20),
        )(mode_shapes.reshape(2, rows, width), mass_blocks, block_cols, send_lists)

    return jax.shard_map(
        local,
        mesh=mesh,
        in_specs=(
            P("sweep", None, "dof", None),
            P(None, None, None, "dof"),
            P(None, "dof"),
            P("dof", None, None),
        ),
        out_specs=P("dof", "sweep", None),
        check_vma=False,
    )
```
